128 devices in a mesh: ranks: 128 (over x, y, z, core).
Axes of the slice: x: 4, y: 4, z: 4, core: 2. Of those that a mesh axis runs over, the one named last changes fastest.
Arguments:
- positions: float32 [3, 4096, 128], P(None, 'ranks'), may hold values from 0 to 1
- velocities: float32 [3, 4096, 128], P(None, 'ranks'), may hold values from -6 to 6
- masses: float32 [4096, 128], P('ranks'), may hold values from 0.001 to 0.004
- smoothing: float32 [4096, 128], P('ranks'), may hold values from 0.35 to 0.7
- energy: float32 [4096, 128], P('ranks'), may hold values from 0.3 to 3
- counts: int32 [4096], P('ranks'), may hold values from 1 to 128, as said below
- active: int32 [4096, 128], P('ranks'), may hold values 0 or 1
- requests: int32 [128, 6, 4], P('ranks'), may hold values from -1 to 31, as said below
- pairs: int32 [4096, 26], P('ranks'), may hold values from 0 to 55, as said below
Outputs:
- accel: float32 [3, 4096, 128], P(None, 'ranks')
- heating: float32 [4096, 128], P('ranks')
- density: float32 [4096, 128], P('ranks')
- step: float32 [], replicated
The draws below stay inside these ranges and needn't reach their ends.
Inputs may be any that keep to these rules, and one draw needn't show every extreme that they name: `requests`: every entry is -1 or a local cell index of the owner; the non-empty entries of one row are distinct and come first; every device imports exactly 4 cells from at least one owner offset. `pairs`: entries below 32 name local cells; an entry 32 + k * 4 + s appears only where requests[d, k, s] is not -1 for the cell's device d. `counts`: every device has a cell holding 128 particles.
All inputs are finite; a program needn't handle non-finite values. No bound on the sum of `active` on one device may be relied on, other than what follows from the above.
Results may differ from the reference program's by a relative error of at most 0.0003.
Values sent between devices are 32-bit elements; how exact they have to be, the bound alone decides.
No kernel may reach another device: no remote copies, remote signals or barrier semaphores. Data moves between devices by JAX's collectives and lax.ppermute only.
A program may use at most 128 MiB of HBM per device.

```python
import math
import jax
import jax.numpy as jnp
from jax import lax

P_SIZE = 128
CD = 32
NB = 26
CAP = 4
REACH = 3
OFFS = 6
CELLS = 4096
N_RANKS = 128


def plan_imports(key):
    fill_key, pick_key, cell_key = jax.random.split(key, 3)
    filled = jax.random.randint(fill_key, (N_RANKS, OFFS), 0, CAP + 1)
    chosen_slot = jax.random.randint(pick_key, (N_RANKS, 1), 0, OFFS)
    filled = jnp.where(jnp.arange(OFFS)[None, :] == chosen_slot, CAP, filled)
    cell_keys = jax.random.split(cell_key, N_RANKS * OFFS)
    chosen = jax.vmap(lambda sub: jax.random.permutation(sub, CD)[:CAP])(cell_keys).reshape(N_RANKS, OFFS, CAP)
    wanted = jnp.where(jnp.arange(CAP)[None, None, :] < filled[:, :, None], chosen, -1)
    return (wanted.astype(jnp.int32), filled)


def draw_requests(key, part):
    wanted, filled = plan_imports(key)
    return wanted


def draw_pairs(key, part):
    wanted, filled = plan_imports(key)
    key = jax.random.fold_in(key, 11)
    present = (jnp.arange(CAP)[None, None, :] < filled[:, :, None]).astype(jnp.int32).reshape(N_RANKS, OFFS * CAP)
    usable = jnp.concatenate([jnp.ones((N_RANKS, CD), jnp.int32), present], axis=1)
    total = jnp.sum(usable, axis=1)
    target = jax.random.randint(key, (N_RANKS, CD, NB), 0, total[:, None, None])
    running = jnp.cumsum(usable, axis=1)
    picked = jnp.sum((running[:, None, None, :] <= target[..., None]).astype(jnp.int32), axis=-1)
    return picked.reshape(N_RANKS * CD, NB).astype(jnp.int32)


def draw_counts(key, part):
    key = jax.random.fold_in(key, 5)
    size_key, pick_key = jax.random.split(key)
    sizes = jax.random.randint(size_key, (N_RANKS, CD), max(1, P_SIZE // 4), P_SIZE + 1)
    chosen_cell = jax.random.randint(pick_key, (N_RANKS, 1), 0, CD)
    sizes = jnp.where(jnp.arange(CD)[None, :] == chosen_cell, P_SIZE, sizes)
    return sizes.reshape(N_RANKS * CD).astype(jnp.int32)


def with_ends(values, rng, smallest, high):
    place = [jax.random.randint(jax.random.fold_in(rng, axis), (), 0, length) for axis, length in enumerate(values.shape)]
    longest = values.shape.index(max(values.shape))
    neighbour = place[:longest] + [(place[longest] + 1) % values.shape[longest]] + place[longest + 1:]
    return values.at[tuple(place)].set(smallest).at[tuple(neighbour)].set(high)


def shard_levels(stream_key, dims, cuts, smallest, top_value):
    def one(position, shards_of):
        heights = jax.random.uniform(jax.random.fold_in(jax.random.fold_in(stream_key, 6), position), (shards_of,), jnp.float32, smallest / len(cuts), top_value / len(cuts))
        return jnp.repeat(jnp.exp(heights), dims[position] // shards_of).reshape((-1,) + (1,) * (len(dims) - position - 1))

    level = one(*cuts[0])
    for cut in cuts[1:]:
        level = level * one(*cut)
    return level


def scatter_about(stream_key, shape, scale, limit, pieces=(), kind=jnp.bfloat16):
    drawn = scale * jax.random.normal(stream_key, shape, jnp.float32)
    if pieces:
        drawn = drawn * shard_levels(stream_key, shape, pieces, -0.22, 0.18)
    return jnp.clip(drawn, -limit, limit).astype(kind)


def setup_inputs(seed: int = 0) -> dict:
    key_of = jax.random.split(jax.random.key(seed), 10)
    return {
        "positions": jnp.clip(1.0 * jax.random.uniform(key_of[0], (3, CELLS, P_SIZE), jnp.float32) ** shard_levels(key_of[0], (3, CELLS, P_SIZE), ((1, 128),), -0.2, 0.2), 0.0, 1.0),
        "velocities": scatter_about(key_of[1], (3, CELLS, P_SIZE), 1.0, 6.0, ((1, 128),), jnp.float32),
        "masses": jnp.clip(jnp.exp(math.log(0.004) - 1.3862944 * jax.random.uniform(key_of[2], (CELLS, P_SIZE), jnp.float32) ** shard_levels(key_of[2], (CELLS, P_SIZE), ((0, 128),), -0.2, 0.2)), 0.001, 0.004),
        "smoothing": jnp.clip(jnp.exp(math.log(0.7) - 0.6931472 * jax.random.uniform(key_of[3], (CELLS, P_SIZE), jnp.float32) ** shard_levels(key_of[3], (CELLS, P_SIZE), ((0, 128),), -0.2, 0.2)), 0.35, 0.7),
        "energy": jnp.clip(jnp.exp(math.log(3.0) - 2.3025851 * jax.random.uniform(key_of[4], (CELLS, P_SIZE), jnp.float32) ** shard_levels(key_of[4], (CELLS, P_SIZE), ((0, 128),), -0.2, 0.2)), 0.3, 3.0),
        "counts": draw_counts(jax.random.fold_in(key_of[9], 71), 0),
        "active": with_ends((jax.random.randint(key_of[6], (CELLS, P_SIZE), 0, 2) < 1).astype(jnp.int32), jax.random.fold_in(key_of[6], 1), 0, 1),
        "requests": draw_requests(jax.random.fold_in(key_of[9], 71), 0),
        "pairs": draw_pairs(jax.random.fold_in(key_of[9], 71), 0),
    }


KERNEL_NORM = 21.0 / (2.0 * math.pi)
ADIABATIC = 5.0 / 3.0
VISC_ALPHA = 1.0
VISC_BETA = 2.0
COURANT = 0.25
SWITCH_EPS = 0.0001
LARGE_STEP = 10000000000.0
cell_group = 4

def kernel_pair(separation, length):
    dist_sq = lax.optimization_barrier(jnp.sum(separation * separation, axis=0))
    ratio = jnp.sqrt(dist_sq) / length
    remain = jnp.where(ratio < 1.0, 1.0 - ratio, 0.0)
    kernel = KERNEL_NORM / length ** 3 * remain ** 4 * (1.0 + 4.0 * ratio)
    slope = -20.0 * KERNEL_NORM / length ** 5 * remain ** 3
    return (dist_sq, kernel, slope)

def cell_density(x_own, h_own, m_own, v_own, x_far, m_far):
    separation = x_own[:, None, :, None] - x_far[:, :, None, :]
    _, kernel, _ = kernel_pair(separation, h_own[None, :, None])
    return lax.optimization_barrier(jnp.sum(m_far[:, None, :] * kernel, axis=(0, 2))) + (1.0 - v_own) * m_own * KERNEL_NORM / h_own ** 3

def cell_gradient(x_own, vel_own, h_own, c_own, x_far, vel_far, m_far, rho_far):
    separation = x_own[:, None, :, None] - x_far[:, :, None, :]
    _, _, slope = kernel_pair(separation, h_own[None, :, None])
    grad = slope[None] * separation
    velocity_gap = vel_far[:, :, None, :] - vel_own[:, None, :, None]
    factor = (m_far / rho_far)[:, None, :]
    divergence = lax.optimization_barrier(jnp.sum(factor * lax.optimization_barrier(jnp.sum(velocity_gap * grad, axis=0)), axis=(0, 2)))
    curl_a = lax.optimization_barrier(jnp.sum(factor * (velocity_gap[1] * grad[2] - velocity_gap[2] * grad[1]), axis=(0, 2)))
    curl_b = lax.optimization_barrier(jnp.sum(factor * (velocity_gap[2] * grad[0] - velocity_gap[0] * grad[2]), axis=(0, 2)))
    curl_c = lax.optimization_barrier(jnp.sum(factor * (velocity_gap[0] * grad[1] - velocity_gap[1] * grad[0]), axis=(0, 2)))
    curl = jnp.sqrt(curl_a * curl_a + curl_b * curl_b + curl_c * curl_c)
    switch = jnp.abs(divergence) / (jnp.abs(divergence) + curl + SWITCH_EPS * c_own / h_own)
    return (divergence, switch)

def cell_force(x_own, vel_own, h_own, rho_own, u_own, b_own, x_far, vel_far, m_far, h_far, rho_far, u_far, b_far):
    separation = x_own[:, None, :, None] - x_far[:, :, None, :]
    velocity_gap = vel_own[:, None, :, None] - vel_far[:, :, None, :]
    approach = lax.optimization_barrier(jnp.sum(separation * velocity_gap, axis=0))
    dist_sq, _, slope_own = kernel_pair(separation, h_own[None, :, None])
    _, _, slope_far = kernel_pair(separation, h_far[:, None, :])
    press_own = (ADIABATIC - 1.0) * rho_own * u_own
    press_far = (ADIABATIC - 1.0) * rho_far * u_far
    c_own = jnp.sqrt(ADIABATIC * (ADIABATIC - 1.0) * u_own)
    c_far = jnp.sqrt(ADIABATIC * (ADIABATIC - 1.0) * u_far)
    h_mean = 0.5 * (h_own[None, :, None] + h_far[:, None, :])
    mu_pair = h_mean * jnp.minimum(approach, 0.0) / (dist_sq + 0.01 * h_mean * h_mean)
    c_mean = 0.5 * (c_own[None, :, None] + c_far[:, None, :])
    rho_mean = 0.5 * (rho_own[None, :, None] + rho_far[:, None, :])
    b_mean = 0.5 * (b_own[None, :, None] + b_far[:, None, :])
    visc = b_mean * (-VISC_ALPHA * c_mean * mu_pair + VISC_BETA * mu_pair * mu_pair) / rho_mean
    own_term = (press_own / rho_own ** 2)[None, :, None] * slope_own
    coeff = m_far[:, None, :] * (own_term + (press_far / rho_far ** 2)[:, None, :] * slope_far + 0.5 * visc * (slope_own + slope_far))
    acc = -lax.optimization_barrier(jnp.sum(coeff[None] * separation, axis=(1, 3)))
    rate = lax.optimization_barrier(jnp.sum(m_far[:, None, :] * (own_term + 0.25 * visc * (slope_own + slope_far)) * approach, axis=(0, 2)))
    return (acc, rate)

def over_blocks(handler, total):
    grouped = jnp.arange(total, dtype=jnp.int32).reshape(total // cell_group, cell_group)
    result = lax.map(jax.vmap(handler), grouped)
    return jax.tree.map(lambda value: value.reshape((total,) + value.shape[2:]), result)

def reference(positions, velocities, masses, smoothing, energy, counts, active, requests, pairs):
    valid = (jnp.arange(P_SIZE, dtype=jnp.int32)[None, :] < counts[:, None]).astype(jnp.float32)
    weighted = masses * valid
    shifts_list = [k - REACH for k in range(REACH)] + [k + 1 for k in range(REACH)]
    offset_table = jnp.array(shifts_list, dtype=jnp.int32)
    owners = (jnp.arange(N_RANKS, dtype=jnp.int32)[:, None] + offset_table[None, :]) % N_RANKS
    imported = (owners[:, :, None] * CD + jnp.maximum(requests, 0)).reshape(N_RANKS, OFFS * CAP)
    local_cells = jnp.arange(N_RANKS, dtype=jnp.int32)[:, None] * CD + jnp.arange(CD, dtype=jnp.int32)[None, :]
    lookup = jnp.concatenate([local_cells, imported], axis=1).astype(jnp.int32)
    device = jnp.arange(CELLS, dtype=jnp.int32) // CD
    neighbours = jnp.concatenate([jnp.arange(CELLS, dtype=jnp.int32)[:, None], lookup[device[:, None], pairs]], axis=1)
    sound = jnp.sqrt(ADIABATIC * (ADIABATIC - 1.0) * energy)

    def density_of(cell):
        near = neighbours[cell]
        return cell_density(positions[:, cell], smoothing[cell], masses[cell], valid[cell], positions[:, near], weighted[near])
    density = over_blocks(density_of, CELLS)

    def gradient_of(cell):
        near = neighbours[cell]
        return cell_gradient(positions[:, cell], velocities[:, cell], smoothing[cell], sound[cell], positions[:, near], velocities[:, near], weighted[near], density[near])
    divergence, switch = over_blocks(gradient_of, CELLS)

    def force_of(cell):
        near = neighbours[cell]
        return cell_force(positions[:, cell], velocities[:, cell], smoothing[cell], density[cell], energy[cell], switch[cell], positions[:, near], velocities[:, near], weighted[near], smoothing[near], density[near], energy[near], switch[near])
    acc, rate = over_blocks(force_of, CELLS)
    living = valid * (active > 0).astype(jnp.float32)
    step_each = COURANT * smoothing / (sound + 0.6 * (VISC_ALPHA * sound + VISC_BETA * smoothing * jnp.maximum(-divergence, 0.0)))
    step = jnp.min(jnp.where(living > 0, step_each, jnp.float32(LARGE_STEP)))
    accel = acc.transpose(1, 0, 2) * living[None]
    return (accel, rate * living, density, step)
```

```python
import functools
import math

import jax
import jax.numpy as jnp
from jax import lax
from jax.experimental import pallas as pl
from jax.experimental.pallas import tpu as pltpu
from jax.sharding import PartitionSpec as P

KERNEL_NORM = 21.0 / (2.0 * math.pi)
ADIABATIC = 5.0 / 3.0
SWITCH_EPS = 0.0001
LARGE_STEP = 10000000000.0
TINY = 1e-12

CD = 32
WIDTH = 128
OFFS = 6
CAP = 4
SLOTS = CD + OFFS * CAP
DUMMY = SLOTS
TABLE = SLOTS + 1
GROUP = 8
LIST = 32
ROWS_ALL = (32, 48, 64, 128)
ROWS_VALID = (64, 96, 128)
SHIFTS = (-3, -2, -1, 1, 2, 3)
F32 = jnp.float32
BF16 = jnp.bfloat16

X, V, M, H, U = 0, 3, 6, 7, 8
CHANNELS = 16


def from_ahead(block, distance):
    count = lax.axis_size("ranks")
    route = [((i + distance) % count, i) for i in range(count)]
    return lax.ppermute(block, "ranks", route)


def halves(value):
    high = value.astype(BF16).astype(F32)
    return high, value - high


def thirds(value):
    high, rest = halves(value)
    middle, low = halves(rest)
    return high, middle, low


def stacked(rows):
    return jnp.concatenate(rows, axis=0)


def left_six(value):
    a, b, c = thirds(value)
    return stacked([a, a, b, b, a, c])


def right_six(value):
    a, b, c = thirds(value)
    return stacked([a, b, a, b, c, a])


def dot_rows(left, right):
    return lax.dot_general(left, right, (((1,), (1,)), ((), ())), preferred_element_type=F32)


def dot_plain(left, right):
    return lax.dot_general(left, right, (((1,), (0,)), ((), ())), preferred_element_type=F32)


def each_slot(requests, local, remote):
    @pl.loop(0, CD // 4)
    def _(step):
        for n in range(4):
            local(step * 4 + n)

    for k in range(OFFS):
        for n in range(CAP):
            remote(k, CD + k * CAP + n, jnp.maximum(requests[k * CAP + n], 0))


def advance(lengths, place):
    position, index = place
    done = index + GROUP >= lengths[position]
    after = jnp.where(done, position + 1, position)
    return jnp.minimum(after, CD), jnp.where(done, 0, index + GROUP)


def side_by_side(array, slots, base):
    return jnp.concatenate([array[slots[base + n]] for n in range(GROUP)], axis=1)


def density_kernel(
    requests, lengths, slots, repeats, state, far0, far1, far2, far3, far4, far5, own, valid,
    density, table, right, left, d0, d1, total,
):
    far = (far0, far1, far2, far3, far4, far5)

    def fill(source, cell, slot):
        rows = stacked([source[c, pl.ds(cell, 1), :] for c in range(9)])
        place = rows[0:3] - 0.5
        norm = jnp.sum(place * place, axis=0, keepdims=True)
        table[slot] = stacked([place, rows[3:9], jnp.zeros((7, WIDTH), F32)])
        one = jnp.ones((1, WIDTH), F32)
        blank = jnp.zeros((3, WIDTH), F32)
        right[slot] = right_six(stacked([-2.0 * place, one, norm, blank])).astype(BF16)
        return place, norm, rows[H : H + 1], one, blank

    def local(s):
        place, norm, length, one, blank = fill(state, s, s)
        scale = 1.0 / (length * length)
        tall = left_six(stacked([place * scale, norm * scale, scale, blank]))
        left[s] = tall.T.astype(BF16)
        total[s] = jnp.zeros((WIDTH, WIDTH), F32)

    each_slot(requests, local, lambda k, s, cell: fill(far[k], cell, s))
    total[CD] = jnp.zeros((WIDTH, WIDTH), F32)
    ones = jnp.ones((1, WIDTH), F32)
    table[DUMMY] = stacked([jnp.zeros((7, WIDTH), F32), ones, ones, jnp.zeros((7, WIDTH), F32)])
    right[DUMMY] = jnp.zeros((48, WIDTH), BF16)

    def distances(place, target):
        cell = jnp.minimum(place[0], CD - 1)
        target[...] = dot_plain(left[cell], side_by_side(right, slots, place[0] * LIST + place[1]))

    def gather(place, source):
        base = place[0] * LIST + place[1]
        masses = [
            table[slots[base + n], M : M + 1, :] * repeats[base + n] for n in range(GROUP)
        ]
        for start in range(0, WIDTH, 16):
            rows = slice(start, start + 16)
            result = total[place[0], rows, :]
            for n in range(GROUP):
                square = jnp.maximum(source[rows, n * WIDTH : (n + 1) * WIDTH], TINY)
                rest = jnp.maximum(1.0 - square * lax.rsqrt(square), 0.0)
                second = rest * rest
                result += second * second * (1.25 - rest) * masses[n]
            total[place[0], rows, :] = result

    units = lengths[CD + 1]
    first = (jnp.int32(0), jnp.int32(0))
    distances(first, d0)

    def step(_, place):
        second = advance(lengths, place)
        third = advance(lengths, second)
        distances(second, d1)
        gather(place, d0)
        distances(third, d0)
        gather(second, d1)
        return third

    lax.fori_loop(0, (units + 1) // 2, step, first)

    @pl.loop(0, CD // 4)
    def _(step):
        for n in range(4):
            cell = step * 4 + n
            density[pl.ds(cell, 1), :] = jnp.sum(total[cell].T, axis=0, keepdims=True)

    length = state[H]
    cube = KERNEL_NORM / (length * length * length)
    density[...] = cube * (4.0 * density[...] + (1.0 - valid[...]) * own[...])


def gradient_kernel(
    requests, lengths, slots, repeats, sizes, order, table, right, left, density,
    far0, far1, far2, far3, far4, far5, live,
    switch, first_terms, smallest,
    feature, d0, d1, a0, a1, total, sums,
):
    far = (far0, far1, far2, far3, far4, far5)

    def fill(source, cell, slot):
        rows = table[slot]
        place, speed, mass = rows[0:3], rows[3:6], rows[M : M + 1]
        light = mass / source[pl.ds(cell, 1), :]
        along = jnp.sum(place * speed, axis=0, keepdims=True)
        x, y, z = rows[0:1], rows[1:2], rows[2:3]
        p, q, r = rows[3:4], rows[4:5], rows[5:6]
        cross = stacked([q * z - r * y, r * x - p * z, p * y - q * x])
        one = jnp.ones((1, WIDTH), F32)
        base = stacked([one, place, speed, along])
        whole = stacked([base * light, base * mass, cross * light, jnp.zeros((5, WIDTH), F32)])
        high, low = halves(whole)
        feature[slot] = stacked([high, low]).T.astype(BF16)

    def local(s):
        fill(density, s, s)
        total[s] = jnp.zeros((WIDTH, 48), F32)

    each_slot(requests, local, lambda k, s, cell: fill(far[k], cell, s))
    total[CD] = jnp.zeros((WIDTH, 48), F32)
    feature[DUMMY] = jnp.zeros((WIDTH, 48), BF16)
    a0[...] = jnp.zeros_like(a0)
    a1[...] = jnp.zeros_like(a1)

    def distances(place, target):
        cell = order[place[0]]
        pair = side_by_side(right, slots, cell * LIST + place[1])
        target[...] = dot_plain(left[jnp.minimum(cell, CD - 1)], pair)

    def collect(place, source, rows):
        cell = order[place[0]]
        base = cell * LIST + place[1]
        both = jnp.concatenate([source[0:rows, :], source[WIDTH : WIDTH + rows, :]], axis=0)
        light = jnp.concatenate([feature[slots[base + n]] for n in range(GROUP)], axis=0)
        both = dot_plain(both, light)
        total[cell, 0:rows, :] += both[:rows] + both[rows:]

    def slopes(place, source, target, rows):
        base = order[place[0]] * LIST + place[1]
        for start in range(0, rows, 16):
            band = slice(start, start + 16)
            below = slice(WIDTH + start, WIDTH + start + 16)
            for n in range(GROUP):
                at = slice(n * WIDTH, (n + 1) * WIDTH)
                square = jnp.maximum(source[band, at], TINY)
                rest = jnp.maximum(1.0 - square * lax.rsqrt(square), 0.0)
                value = rest * rest * (rest * repeats[base + n])
                high = value.astype(BF16)
                target[band, at] = high
                target[below, at] = (value - high.astype(F32)).astype(BF16)

    units = lengths[CD + 1]
    place = (jnp.int32(0), jnp.int32(0))
    before = (jnp.int32(CD), jnp.int32(0))
    distances(place, d0)

    def half(last, place, after, d_now, d_next, a_last, a_now):
        def body(rows):
            distances(after, d_next)
            collect(last, a_last, rows)
            slopes(place, d_now, a_now, rows)

        branch(jnp.maximum(sizes[order[last[0]]], sizes[order[place[0]]]), ROWS_VALID, body)

    def step(_, carry):
        last, place = carry
        second = advance_in(order, lengths, place)
        third = advance_in(order, lengths, second)
        half(last, place, second, d0, d1, a1, a0)
        half(place, second, third, d1, d0, a0, a1)
        return second, third

    last, _ = lax.fori_loop(0, (units + 1) // 2, step, (before, place))
    collect(last, a1, WIDTH)

    @pl.loop(0, CD // 4)
    def _(step):
        for n in range(4):
            cell = step * 4 + n
            tall = total[cell].T
            sums[:, pl.ds(cell, 1), :] = (tall[0:24] + tall[24:48]).reshape(24, 1, WIDTH)

    x = [table[0:CD, c, :] for c in range(3)]
    v = [table[0:CD, 3 + c, :] for c in range(3)]
    length = table[0:CD, H, :]
    energy = table[0:CD, U, :]
    rho = density[...]
    along = x[0] * v[0] + x[1] * v[1] + x[2] * v[2]

    def approach(at):
        value = along * sums[at] + sums[at + 7]
        for c in range(3):
            value = value - x[c] * sums[at + 4 + c] - v[c] * sums[at + 1 + c]
        return value

    square = length * length
    slope = (-20.0 * KERNEL_NORM) / (square * square * length)
    divergence = -slope * approach(0)
    curl = jnp.zeros_like(divergence)
    for c in range(3):
        e, f = (c + 1) % 3, (c + 2) % 3
        part = (
            sums[4 + e] * x[f] - sums[4 + f] * x[e] - sums[16 + c]
            - sums[0] * (v[e] * x[f] - v[f] * x[e])
            + v[e] * sums[1 + f] - v[f] * sums[1 + e]
        )
        curl = curl + part * part
    curl = jnp.sqrt(curl) * jnp.abs(slope)
    sound = jnp.sqrt((ADIABATIC * (ADIABATIC - 1.0)) * energy)
    size = jnp.abs(divergence)
    switch[...] = size / (size + curl + SWITCH_EPS * sound / length)
    ratio = (ADIABATIC - 1.0) * energy / rho * slope
    for c in range(3):
        first_terms[c] = -ratio * (x[c] * sums[8] - sums[9 + c])
    first_terms[3] = ratio * approach(8)
    each = 0.25 * length / (
        sound + 0.6 * (sound + 2.0 * length * jnp.maximum(-divergence, 0.0))
    )
    each = jnp.where(live[...] > 0, each, LARGE_STEP)
    smallest[...] = jnp.broadcast_to(jnp.min(each, keepdims=True), (8, WIDTH))


def branch(need, options, body):
    which = jnp.int32(0)
    for option in options[:-1]:
        which += (need > option).astype(jnp.int32)
    lax.switch(which, [functools.partial(body, option) for option in options])


def advance_in(order, lengths, place):
    position, index = place
    done = index + GROUP >= lengths[order[position]]
    after = jnp.where(done, position + 1, position)
    return jnp.minimum(after, CD), jnp.where(done, 0, index + GROUP)


def force_kernel(
    requests, lengths, slots, repeats, sizes, order, table, right, density,
    rho0, rho1, rho2, rho3, rho4, rho5, switch, sw0, sw1, sw2, sw3, sw4, sw5, live, first_terms,
    accel, heating,
    other, line, left, chosen, column, d0, d1, total, sums,
):
    rho_far = (rho0, rho1, rho2, rho3, rho4, rho5)
    switch_far = (sw0, sw1, sw2, sw3, sw4, sw5)
    one = jnp.ones((1, WIDTH), F32)

    def fill(rho_source, switch_source, cell, slot):
        rows = table[slot]
        place, speed, mass = rows[0:3], rows[3:6], rows[M : M + 1]
        length, energy = rows[H : H + 1], rows[U : U + 1]
        rho = rho_source[pl.ds(cell, 1), :]
        bulk = switch_source[pl.ds(cell, 1), :]
        along = jnp.sum(place * speed, axis=0, keepdims=True)
        square = length * length
        fourth = square * square
        slope = (-20.0 * KERNEL_NORM) / (fourth * fourth)
        sound = jnp.sqrt((ADIABATIC * (ADIABATIC - 1.0)) * energy)
        push = (ADIABATIC - 1.0) * energy / rho * mass
        values = stacked(
            [length, slope, 0.05 * length, sound * 0.025, rho, 100.0 * bulk, mass, push]
        )
        line[slot] = stacked([values, place, jnp.zeros((5, WIDTH), F32)])
        a, b = halves(stacked([-speed, -place, one, along]))
        other[slot] = stacked([a, b, a, b]).astype(BF16)
        return place, speed, along, values

    alive = live[...]
    down = lax.broadcasted_iota(jnp.int32, (WIDTH, WIDTH), 0)
    across = lax.broadcasted_iota(jnp.int32, (WIDTH, WIDTH), 1)
    earlier = jnp.where(down < across, 1.0, 0.0).astype(BF16)
    rank = dot_plain(alive.astype(BF16), earlier)
    sums[0] = jnp.where(alive > 0, rank, -1.0)

    def local(s):
        place, speed, along, values = fill(density, switch, s, s)
        norm = jnp.sum(place * place, axis=0, keepdims=True)
        near = left_six(stacked([place, norm, one, jnp.zeros((3, WIDTH), F32)]))
        a, b = halves(stacked([place, speed, along, one]))
        high, middle, low = thirds(values)
        tall = stacked([near, a, a, b, b, high, middle, low, jnp.zeros((24, WIDTH), F32)]).astype(BF16)
        pick = jnp.where(sums[0, pl.ds(s, 1), :] == down.astype(F32), 1.0, 0.0).astype(BF16)
        chosen[s] = pick
        moved = dot_rows(pick, tall)
        left[s] = moved.astype(BF16)
        column[s] = moved[:, 80:88] + moved[:, 88:96] + moved[:, 96:104]
        total[s] = jnp.zeros((5, WIDTH, WIDTH), F32)

    each_slot(
        requests, local, lambda k, s, cell: fill(rho_far[k], switch_far[k], cell, s)
    )
    total[CD] = jnp.zeros((5, WIDTH, WIDTH), F32)
    column[CD] = jnp.ones((WIDTH, 8), F32)
    line[DUMMY] = jnp.ones((16, WIDTH), F32)
    other[DUMMY] = jnp.zeros((32, WIDTH), BF16)

    def distances(place, target, rows):
        cell = order[place[0]]
        base = cell * LIST + place[1]
        cell = jnp.minimum(cell, CD - 1)
        width = GROUP * WIDTH
        target[0:rows, :width] = dot_plain(
            left[cell, 0:rows, 0:48], side_by_side(right, slots, base)
        )
        target[0:rows, width:] = dot_plain(
            left[cell, 0:rows, 48:80], side_by_side(other, slots, base)
        )

    def pair_terms(place, source, rows):
        cell = order[place[0]]
        base = cell * LIST + place[1]
        for start in range(0, rows, 16):
            band = slice(start, start + 16)
            own = column[cell, band, :]
            h_i, s_i, k_i, c_i, rho_i, b_i = [
                jnp.broadcast_to(own[:, c : c + 1], (16, WIDTH)) for c in range(6)
            ]
            result = [total[cell, c, band, :] for c in range(5)]
            for n in range(GROUP):
                rows_j = line[slots[base + n]]
                h_j, s_j, k_j, c_j, rho_j, b_j = [rows_j[c : c + 1] for c in range(6)]
                mass = rows_j[6:7] * repeats[base + n]
                push = rows_j[7:8] * repeats[base + n]
                square = jnp.maximum(source[band, n * WIDTH : (n + 1) * WIDTH], TINY)
                at = (GROUP + n) * WIDTH
                closing = source[band, at : at + WIDTH]
                dist = square * lax.rsqrt(square)
                t_i = jnp.maximum(h_i - dist, 0.0)
                t_j = jnp.maximum(h_j - dist, 0.0)
                g_i = t_i * t_i * t_i * s_i
                g_j = t_j * t_j * t_j * s_j
                k = k_i + k_j
                near = k * jnp.minimum(closing, 0.0)
                wide = square + k * k
                top = near * (near - wide * (c_i + c_j)) * (b_i + b_j)
                under = pltpu.reciprocal(wide * wide * (rho_i + rho_j), approx=True)
                v = top * under * (g_i + g_j) * mass
                both = v + g_j * push
                result[0] += both
                for c in range(3):
                    result[1 + c] += both * rows_j[8 + c : 9 + c]
                result[4] += v * closing
            for c in range(5):
                total[cell, c, band, :] = result[c]

    units = lengths[CD + 1]
    first = (jnp.int32(0), jnp.int32(0))
    distances(first, d0, WIDTH)

    def half(place, after, d_now, d_next):
        need = sizes[order[place[0]]]
        need = jnp.where(sizes[order[after[0]]] > 64, WIDTH, need)

        def body(rows):
            distances(after, d_next, max(rows, 64))
            pair_terms(place, d_now, rows)

        branch(need, ROWS_ALL, body)

    def step(_, place):
        second = advance_in(order, lengths, place)
        third = advance_in(order, lengths, second)
        half(place, second, d0, d1)
        half(second, third, d1, d0)
        return third

    lax.fori_loop(0, (units + 1) // 2, step, first)

    @pl.loop(0, CD // 2)
    def _(step):
        for n in range(2):
            cell = step * 2 + n
            pick = chosen[cell].astype(F32)
            back = [
                jnp.sum(
                    jnp.sum(total[cell, c], axis=1, keepdims=True) * pick, axis=0, keepdims=True
                )
                for c in range(5)
            ]
            sums[:, pl.ds(cell, 1), :] = stacked(back).reshape(5, 1, WIDTH)

    x = [table[0:CD, c, :] for c in range(3)]
    v = [table[0:CD, 3 + c, :] for c in range(3)]
    along = x[0] * v[0] + x[1] * v[1] + x[2] * v[2]
    for c in range(3):
        inner = x[c] * sums[0] - sums[1 + c]
        accel[c] = (first_terms[c] - inner) * alive
    heating[...] = (first_terms[3] + 0.5 * sums[4]) * alive


def call(kernel, scalars, arrays, outs, scratch, name):
    smem = pl.BlockSpec(memory_space=pltpu.SMEM)
    vmem = pl.BlockSpec(memory_space=pltpu.VMEM)
    return pl.pallas_call(
        kernel,
        out_shape=[jax.ShapeDtypeStruct(shape, kind) for shape, kind in outs],
        in_specs=[smem] * len(scalars) + [vmem] * len(arrays),
        out_specs=[vmem] * len(outs),
        scratch_shapes=[pltpu.VMEM(shape, kind) for shape, kind in scratch],
        compiler_params=pltpu.CompilerParams(vmem_limit_bytes=48 * 1024 * 1024),
        name=name,
    )(*scalars, *arrays)


def partner_lists(pairs):
    cells = jnp.arange(CD, dtype=jnp.int32)[:, None]
    every = jnp.concatenate([cells, pairs], axis=1)
    slot = jnp.arange(SLOTS, dtype=jnp.int32)
    repeats = jnp.sum((every[:, :, None] == slot).astype(jnp.int32), axis=1)
    present = repeats > 0
    before = (slot[:, None] < slot[None, :]).astype(jnp.int32)
    rank = jnp.sum(present.astype(jnp.int32)[:, :, None] * before[None], axis=1)
    length = jnp.sum(present.astype(jnp.int32), axis=1)
    place = jnp.arange(LIST, dtype=jnp.int32)
    hit = (present[:, :, None] & (rank[:, :, None] == place)).astype(jnp.int32)
    slots = jnp.sum(hit * slot[None, :, None], axis=1)
    slots = jnp.where(place[None, :] < length[:, None], slots, DUMMY)
    repeats = jnp.sum(hit * repeats[:, :, None], axis=1)
    slots = jnp.concatenate([slots, jnp.full((1, LIST), DUMMY, jnp.int32)])
    repeats = jnp.concatenate([repeats, jnp.zeros((1, LIST), jnp.int32)])
    units = jnp.sum((length + GROUP - 1) // GROUP)
    none = jnp.zeros((1,), jnp.int32)
    lengths = jnp.concatenate([length, none, units[None]])
    return lengths, slots.reshape(-1), repeats.reshape(-1).astype(F32)


def descending(sizes):
    cell = jnp.arange(CD, dtype=jnp.int32)
    ahead = (sizes[None, :] > sizes[:, None]) | (
        (sizes[None, :] == sizes[:, None]) & (cell[None, :] < cell[:, None])
    )
    rank = jnp.sum(ahead.astype(jnp.int32), axis=1)
    order = jnp.sum(jnp.where(rank[None, :] == cell[:, None], cell[None, :], 0), axis=1)
    return jnp.concatenate([order, jnp.full((1,), CD, jnp.int32)])


def on_device(positions, velocities, masses, smoothing, energy, counts, active, requests, pairs):
    valid = (jnp.arange(WIDTH, dtype=jnp.int32)[None, :] < counts[:, None]).astype(F32)
    live = valid * (active > 0).astype(F32)
    weighted = masses * valid
    state = jnp.concatenate(
        [positions, velocities, weighted[None], smoothing[None], energy[None]], axis=0
    )
    far = [from_ahead(state, d) for d in SHIFTS]
    wanted = requests.reshape(-1)
    lengths, slots, repeats = partner_lists(pairs)
    scalars = (wanted, lengths, slots, repeats)
    none = jnp.zeros((1,), jnp.int32)
    count_sizes = jnp.concatenate([counts, none])
    live_sizes = jnp.concatenate([jnp.sum(live, axis=1).astype(jnp.int32), none])

    density, table, right, left = call(
        density_kernel, scalars, (state, *far, masses, valid),
        [((CD, WIDTH), F32), ((TABLE, CHANNELS, WIDTH), F32), ((TABLE, 48, WIDTH), BF16),
         ((CD, WIDTH, 48), BF16)],
        [((WIDTH, GROUP * WIDTH), F32)] * 2 + [((CD + 1, WIDTH, WIDTH), F32)],
        "density",
    )
    rho_far = [from_ahead(density, d) for d in SHIFTS]
    switch, first_terms, smallest = call(
        gradient_kernel, (*scalars, count_sizes, descending(counts)), (table, right, left, density, *rho_far, live),
        [((CD, WIDTH), F32), ((4, CD, WIDTH), F32), ((8, WIDTH), F32)],
        [((TABLE, WIDTH, 48), BF16)] + [((WIDTH, GROUP * WIDTH), F32)] * 2
        + [((2 * WIDTH, GROUP * WIDTH), BF16)] * 2
        + [((CD + 1, WIDTH, 48), F32), ((24, CD, WIDTH), F32)],
        "gradient",
    )
    packed = jnp.concatenate([switch, smallest], axis=0)
    switch_far = [from_ahead(packed, d) for d in SHIFTS]
    for block in switch_far:
        smallest = jnp.minimum(smallest, block[CD:])
    for distance in (7, 14, 28, 56, 112):
        smallest = jnp.minimum(smallest, from_ahead(smallest, distance))
    accel, heating = call(
        force_kernel, (*scalars, live_sizes, descending(live_sizes[:CD])),
        (table, right, density, *rho_far, switch, *switch_far, live, first_terms),
        [((3, CD, WIDTH), F32), ((CD, WIDTH), F32)],
        [((TABLE, 32, WIDTH), BF16), ((TABLE, 16, WIDTH), F32),
         ((CD, WIDTH, WIDTH), BF16), ((CD, WIDTH, WIDTH), BF16), ((CD + 1, WIDTH, 8), F32)]
        + [((WIDTH, 2 * GROUP * WIDTH), F32)] * 2
        + [((CD + 1, 5, WIDTH, WIDTH), F32), ((5, CD, WIDTH), F32)],
        "force",
    )
    return accel, heating, density, smallest[0, 0]


def solution(mesh):
    in_specs = (
        P(None, "ranks", None),
        P(None, "ranks", None),
        P("ranks", None),
        P("ranks", None),
        P("ranks", None),
        P("ranks"),
        P("ranks", None),
        P("ranks", None, None),
        P("ranks", None),
    )
    out_specs = (P(None, "ranks", None), P("ranks", None), P("ranks", None), P())
    return jax.shard_map(
        on_device, mesh=mesh, in_specs=in_specs, out_specs=out_specs, check_vma=False
    )
```

```python
import functools
import math

import jax
import jax.numpy as jnp
from jax import lax
from jax.experimental import pallas as pl
from jax.experimental.pallas import tpu as pltpu
from jax.sharding import PartitionSpec as P

KERNEL_NORM = 21.0 / (2.0 * math.pi)
ADIABATIC = 5.0 / 3.0
SWITCH_EPS = 0.0001
LARGE_STEP = 10000000000.0
TINY = 1e-12

CD = 32
WIDTH = 128
OFFS = 6
CAP = 4
SLOTS = CD + OFFS * CAP
DUMMY = SLOTS
TABLE = SLOTS + 1
PARTS = 4
PART = WIDTH // PARTS
GROUP = 9
LIST = 27 * PARTS
HALF = CD // 2
ROWS_ALL = (32, 48, 64, 128)
ROWS_VALID = (64, 96, 128)
SHIFTS = (-3, -2, -1, 1, 2, 3)
F32 = jnp.float32
BF16 = jnp.bfloat16

X, V, M, H, U = 0, 3, 6, 7, 8
CHANNELS = 16


def from_ahead(block, distance):
    count = lax.axis_size("ranks")
    route = [((i + distance) % count, i) for i in range(count)]
    return lax.ppermute(block, "ranks", route)


def halves(value):
    high = value.astype(BF16).astype(F32)
    return high, value - high


def thirds(value):
    high, rest = halves(value)
    middle, low = halves(rest)
    return high, middle, low


def stacked(rows):
    return jnp.concatenate(rows, axis=0)


def left_six(value):
    a, b, c = thirds(value)
    return stacked([a, a, b, b, a, c])


def right_six(value):
    a, b, c = thirds(value)
    return stacked([a, b, a, b, c, a])


def dot_rows(left, right):
    return lax.dot_general(left, right, (((1,), (1,)), ((), ())), preferred_element_type=F32)


def dot_plain(left, right):
    return lax.dot_general(left, right, (((1,), (0,)), ((), ())), preferred_element_type=F32)


def each_slot(requests, local, remote):
    @pl.loop(0, CD // 4)
    def _(step):
        for n in range(4):
            local(step * 4 + n)

    for k in range(OFFS):
        for n in range(CAP):
            remote(k, CD + k * CAP + n, jnp.maximum(requests[k * CAP + n], 0))


def advance(order, lengths, place):
    position, index = place
    cell = jnp.minimum(order[position], CD - 1)
    done = index + GROUP >= lengths[cell]
    after = jnp.where(done, position + 1, position)
    return jnp.minimum(after, CD), jnp.where(done, 0, index + GROUP)


def count_units(lengths, low, high):
    def add(cell, total):
        return total + (lengths[cell] + (GROUP - 1)) // GROUP

    return lax.fori_loop(low, high, add, jnp.int32(0))


def entries(codes, cell, index):
    base = cell * LIST + index * PARTS
    found = []
    for n in range(GROUP):
        four = [codes[base + n * PARTS + p] for p in range(PARTS)]
        found.append([(c & 255, (c >> 8) & 255, (c >> 16).astype(F32)) for c in four])
    return found


def part_masks(rows, kind):
    lane = lax.broadcasted_iota(jnp.int32, (rows, WIDTH), 1)
    return [((lane >= PART * p) & (lane < PART * (p + 1))).astype(F32).astype(kind) for p in range(PARTS)]


def tile_of(array, four, masks):
    result = array[four[0][0]] * masks[0]
    for p in range(1, PARTS):
        result += array[four[p][0]] * masks[p]
    return result


def count_line(four):
    lane = lax.broadcasted_iota(jnp.int32, (1, WIDTH), 1)
    result = jnp.full((1, WIDTH), four[0][2], F32)
    for p in range(1, PARTS):
        result = jnp.where(lane >= PART * p, four[p][2], result)
    return result


def side_by_side(array, units, rows):
    masks = part_masks(rows, BF16)
    return jnp.concatenate([tile_of(array, four, masks) for four in units], axis=1)


def turned(value):
    return [value] + [pltpu.roll(value, PART * p, 1) for p in range(1, PARTS)]


def density_kernel(
    requests, lengths, codes, state, far0, far1, far2, far3, far4, far5, own, valid,
    density, table, right, left, weight, d0, d1, total,
):
    far = (far0, far1, far2, far3, far4, far5)

    def fill(source, cell, slot):
        rows = stacked([source[c, pl.ds(cell, 1), :] for c in range(9)])
        place = rows[0:3] - 0.5
        norm = jnp.sum(place * place, axis=0, keepdims=True)
        table[slot] = stacked([place, rows[3:9], jnp.zeros((7, WIDTH), F32)])
        one = jnp.ones((1, WIDTH), F32)
        blank = jnp.zeros((3, WIDTH), F32)
        for p, value in enumerate(turned(stacked([-2.0 * place, one, norm, blank]))):
            right[slot * PARTS + p] = right_six(value).astype(BF16)
        for p, value in enumerate(turned(rows[0:8])):
            weight[slot * PARTS + p] = value
        return place, norm, rows[H : H + 1], one, blank

    def local(s):
        place, norm, length, one, blank = fill(state, s, s)
        scale = 1.0 / (length * length)
        tall = left_six(stacked([place * scale, norm * scale, scale, blank]))
        left[s] = tall.T.astype(BF16)
        total[s] = jnp.zeros((WIDTH, WIDTH), F32)

    each_slot(requests, local, lambda k, s, cell: fill(far[k], cell, s))
    total[CD] = jnp.zeros((WIDTH, WIDTH), F32)
    ones = jnp.ones((1, WIDTH), F32)
    table[DUMMY] = stacked([jnp.zeros((7, WIDTH), F32), ones, ones, jnp.zeros((7, WIDTH), F32)])
    for p in range(PARTS):
        right[DUMMY * PARTS + p] = jnp.zeros((48, WIDTH), BF16)
        weight[DUMMY * PARTS + p] = jnp.zeros((8, WIDTH), F32)

    def distances(place, target):
        cell = jnp.minimum(place[0], CD - 1)
        units = entries(codes, place[0], place[1])
        target[...] = dot_plain(left[cell], side_by_side(right, units, 48))

    masks = part_masks(8, F32)

    def gather(place, source):
        units = entries(codes, place[0], place[1])
        masses = [
            tile_of(weight, four, masks)[M : M + 1, :] * count_line(four) for four in units
        ]
        for start in range(0, WIDTH, 16):
            rows = slice(start, start + 16)
            result = total[place[0], rows, :]
            for n in range(GROUP):
                square = jnp.maximum(source[rows, n * WIDTH : (n + 1) * WIDTH], TINY)
                rest = jnp.maximum(1.0 - square * lax.rsqrt(square), 0.0)
                second = rest * rest
                result += second * second * (1.25 - rest) * masses[n]
            total[place[0], rows, :] = result

    units = count_units(lengths, 0, CD)
    first = (jnp.int32(0), jnp.int32(0))
    distances(first, d0)

    def following(place):
        cell, index = place
        done = index + GROUP >= lengths[jnp.minimum(cell, CD - 1)]
        return jnp.minimum(jnp.where(done, cell + 1, cell), CD), jnp.where(done, 0, index + GROUP)

    def step(_, place):
        second = following(place)
        third = following(second)
        distances(second, d1)
        gather(place, d0)
        distances(third, d0)
        gather(second, d1)
        return third

    lax.fori_loop(0, (units + 1) // 2, step, first)

    @pl.loop(0, CD // 4)
    def _(step):
        for n in range(4):
            cell = step * 4 + n
            density[pl.ds(cell, 1), :] = jnp.sum(total[cell].T, axis=0, keepdims=True)

    length = state[H]
    cube = KERNEL_NORM / (length * length * length)
    density[...] = cube * (4.0 * density[...] + (1.0 - valid[...]) * own[...])


def gradient_kernel(
    requests, lengths, codes, sizes, order, table, right, left, density,
    far0, far1, far2, far3, far4, far5, live,
    switch, first_terms, smallest,
    feature, d0, d1, a0, a1, total, sums,
):
    far = (far0, far1, far2, far3, far4, far5)

    def fill(source, cell, slot):
        rows = table[slot]
        place, speed, mass = rows[0:3], rows[3:6], rows[M : M + 1]
        light = mass / source[pl.ds(cell, 1), :]
        along = jnp.sum(place * speed, axis=0, keepdims=True)
        x, y, z = rows[0:1], rows[1:2], rows[2:3]
        p, q, r = rows[3:4], rows[4:5], rows[5:6]
        cross = stacked([q * z - r * y, r * x - p * z, p * y - q * x])
        one = jnp.ones((1, WIDTH), F32)
        base = stacked([one, place, speed, along])
        whole = stacked([base * light, base * mass, cross * light, jnp.zeros((5, WIDTH), F32)])
        high, low = halves(whole)
        tall = stacked([high, low]).T.astype(BF16)
        for p in range(PARTS):
            feature[slot * PARTS + p] = tall[PART * p : PART * (p + 1)]

    def local(s):
        fill(density, s, s)
        total[s] = jnp.zeros((WIDTH, 48), F32)

    each_slot(requests, local, lambda k, s, cell: fill(far[k], cell, s))
    total[CD] = jnp.zeros((WIDTH, 48), F32)
    for p in range(PARTS):
        feature[DUMMY * PARTS + p] = jnp.zeros((PART, 48), BF16)
    a0[...] = jnp.zeros_like(a0)
    a1[...] = jnp.zeros_like(a1)

    def distances(place, target):
        cell = order[place[0]]
        pair = side_by_side(right, entries(codes, cell, place[1]), 48)
        target[...] = dot_plain(left[jnp.minimum(cell, CD - 1)], pair)

    def collect(place, source, rows):
        cell = order[place[0]]
        units = entries(codes, cell, place[1])
        both = jnp.concatenate([source[0:rows, :], source[WIDTH : WIDTH + rows, :]], axis=0)
        light = jnp.concatenate([feature[e[1]] for four in units for e in four], axis=0)
        both = dot_plain(both, light)
        total[cell, 0:rows, :] += both[:rows] + both[rows:]

    def slopes(place, source, target, rows):
        units = entries(codes, order[place[0]], place[1])
        counts = [jnp.broadcast_to(count_line(four), (16, WIDTH)) for four in units]
        for start in range(0, rows, 16):
            band = slice(start, start + 16)
            below = slice(WIDTH + start, WIDTH + start + 16)
            for n in range(GROUP):
                at = slice(n * WIDTH, (n + 1) * WIDTH)
                square = jnp.maximum(source[band, at], TINY)
                rest = jnp.maximum(1.0 - square * lax.rsqrt(square), 0.0)
                value = rest * rest * (rest * counts[n])
                high = value.astype(BF16)
                target[band, at] = high
                target[below, at] = (value - high.astype(F32)).astype(BF16)

    units = count_units(lengths, 0, CD)
    place = (jnp.int32(0), jnp.int32(0))
    before = (jnp.int32(CD), jnp.int32(0))
    distances(place, d0)

    def half(last, place, after, d_now, d_next, a_last, a_now):
        def body(rows):
            distances(after, d_next)
            collect(last, a_last, rows)
            slopes(place, d_now, a_now, rows)

        branch(jnp.maximum(sizes[order[last[0]]], sizes[order[place[0]]]), ROWS_VALID, body)

    def step(_, carry):
        last, place = carry
        second = advance(order, lengths, place)
        third = advance(order, lengths, second)
        half(last, place, second, d0, d1, a1, a0)
        half(place, second, third, d1, d0, a0, a1)
        return second, third

    last, _ = lax.fori_loop(0, (units + 1) // 2, step, (before, place))
    collect(last, a1, WIDTH)

    @pl.loop(0, CD // 4)
    def _(step):
        for n in range(4):
            cell = step * 4 + n
            tall = total[cell].T
            sums[:, pl.ds(cell, 1), :] = (tall[0:24] + tall[24:48]).reshape(24, 1, WIDTH)

    x = [table[0:CD, c, :] for c in range(3)]
    v = [table[0:CD, 3 + c, :] for c in range(3)]
    length = table[0:CD, H, :]
    energy = table[0:CD, U, :]
    rho = density[...]
    along = x[0] * v[0] + x[1] * v[1] + x[2] * v[2]

    def approach(at):
        value = along * sums[at] + sums[at + 7]
        for c in range(3):
            value = value - x[c] * sums[at + 4 + c] - v[c] * sums[at + 1 + c]
        return value

    square = length * length
    slope = (-20.0 * KERNEL_NORM) / (square * square * length)
    divergence = -slope * approach(0)
    curl = jnp.zeros_like(divergence)
    for c in range(3):
        e, f = (c + 1) % 3, (c + 2) % 3
        part = (
            sums[4 + e] * x[f] - sums[4 + f] * x[e] - sums[16 + c]
            - sums[0] * (v[e] * x[f] - v[f] * x[e])
            + v[e] * sums[1 + f] - v[f] * sums[1 + e]
        )
        curl = curl + part * part
    curl = jnp.sqrt(curl) * jnp.abs(slope)
    sound = jnp.sqrt((ADIABATIC * (ADIABATIC - 1.0)) * energy)
    size = jnp.abs(divergence)
    switch[...] = size / (size + curl + SWITCH_EPS * sound / length)
    ratio = (ADIABATIC - 1.0) * energy / rho * slope
    for c in range(3):
        first_terms[c] = -ratio * (x[c] * sums[8] - sums[9 + c])
    first_terms[3] = ratio * approach(8)
    each = 0.25 * length / (
        sound + 0.6 * (sound + 2.0 * length * jnp.maximum(-divergence, 0.0))
    )
    each = jnp.where(live[...] > 0, each, LARGE_STEP)
    smallest[...] = jnp.broadcast_to(jnp.min(each, keepdims=True), (8, WIDTH))


def branch(need, options, body):
    which = jnp.int32(0)
    for option in options[:-1]:
        which += (need > option).astype(jnp.int32)
    lax.switch(which, [functools.partial(body, option) for option in options])


def force_kernel(
    first, requests, lengths, codes, sizes, order, table, right, density,
    rho0, rho1, rho2, rho3, rho4, rho5, switch, sw0, sw1, sw2, sw3, sw4, sw5, live, first_terms,
    *rest,
):
    accel, heating, other, line, left, chosen, column, d0, d1, total, sums, ranks = rest[-12:]
    rho_far = (rho0, rho1, rho2, rho3, rho4, rho5)
    switch_far = (sw0, sw1, sw2, sw3, sw4, sw5)
    one = jnp.ones((1, WIDTH), F32)

    def fill(rho_source, switch_source, cell, slot):
        rows = table[slot]
        place, speed, mass = rows[0:3], rows[3:6], rows[M : M + 1]
        length, energy = rows[H : H + 1], rows[U : U + 1]
        rho = rho_source[pl.ds(cell, 1), :]
        bulk = switch_source[pl.ds(cell, 1), :]
        along = jnp.sum(place * speed, axis=0, keepdims=True)
        square = length * length
        fourth = square * square
        slope = (-20.0 * KERNEL_NORM) / (fourth * fourth)
        sound = jnp.sqrt((ADIABATIC * (ADIABATIC - 1.0)) * energy)
        push = (ADIABATIC - 1.0) * energy / rho * mass
        values = stacked(
            [length, slope, 0.05 * length, sound * 0.025, rho, 100.0 * bulk, mass, push]
        )
        for p, value in enumerate(turned(stacked([values, place, jnp.zeros((5, WIDTH), F32)]))):
            line[slot * PARTS + p] = value
        for p, value in enumerate(turned(stacked([-speed, -place, one, along]))):
            a, b = halves(value)
            other[slot * PARTS + p] = stacked([a, b, a, b]).astype(BF16)
        return place, speed, along, values

    alive = live[...]
    down = lax.broadcasted_iota(jnp.int32, (WIDTH, WIDTH), 0)
    across = lax.broadcasted_iota(jnp.int32, (WIDTH, WIDTH), 1)
    earlier = jnp.where(down < across, 1.0, 0.0).astype(BF16)
    rank = dot_plain(alive.astype(BF16), earlier)
    ranks[...] = jnp.where(alive > 0, rank, -1.0)

    def slot_only(s):
        fill(density, switch, s, s)

    def local(n):
        s = first + n
        place, speed, along, values = fill(density, switch, s, s)
        norm = jnp.sum(place * place, axis=0, keepdims=True)
        near = left_six(stacked([place, norm, one, jnp.zeros((3, WIDTH), F32)]))
        a, b = halves(stacked([place, speed, along, one]))
        high, middle, low = thirds(values)
        tall = stacked([near, a, a, b, b, high, middle, low, jnp.zeros((24, WIDTH), F32)]).astype(BF16)
        pick = jnp.where(ranks[pl.ds(s, 1), :] == down.astype(F32), 1.0, 0.0).astype(BF16)
        chosen[n] = pick
        spare = 1.0 - jnp.sum(pick.astype(F32), axis=1, keepdims=True)
        moved = dot_rows(pick, tall)
        left[n] = moved.astype(BF16)
        column[n] = moved[:, 80:88] + moved[:, 88:96] + moved[:, 96:104] + spare
        total[n] = jnp.zeros((5, WIDTH, WIDTH), F32)

    @pl.loop(0, HALF // 4)
    def _(step):
        for n in range(4):
            local(step * 4 + n)
            slot_only(HALF - first + step * 4 + n)

    for k in range(OFFS):
        for n in range(CAP):
            cell = jnp.maximum(requests[k * CAP + n], 0)
            fill(rho_far[k], switch_far[k], cell, CD + k * CAP + n)

    total[HALF] = jnp.zeros((5, WIDTH, WIDTH), F32)
    column[HALF] = jnp.ones((WIDTH, 8), F32)
    for p in range(PARTS):
        line[DUMMY * PARTS + p] = jnp.concatenate(
            [jnp.ones((6, WIDTH), F32), jnp.zeros((10, WIDTH), F32)], axis=0
        )
        other[DUMMY * PARTS + p] = jnp.zeros((32, WIDTH), BF16)

    def distances(place, target, rows):
        cell = order[place[0]]
        units = entries(codes, cell, place[1])
        cell = jnp.minimum(cell - first, HALF - 1)
        width = GROUP * WIDTH
        target[0:rows, :width] = dot_plain(left[cell, 0:rows, 0:48], side_by_side(right, units, 48))
        target[0:rows, width:] = dot_plain(left[cell, 0:rows, 48:80], side_by_side(other, units, 32))

    masks = part_masks(16, F32)

    def pair_terms(place, source, rows):
        cell = order[place[0]]
        units = entries(codes, cell, place[1])
        lines = [tile_of(line, four, masks) for four in units]
        counts = [count_line(four) for four in units]
        cell = jnp.minimum(cell - first, HALF)
        for start in range(0, rows, 16):
            band = slice(start, start + 16)
            own = column[cell, band, :]
            h_i, s_i, k_i, c_i, rho_i, b_i = [
                jnp.broadcast_to(own[:, c : c + 1], (16, WIDTH)) for c in range(6)
            ]
            result = [total[cell, c, band, :] for c in range(5)]
            for n in range(GROUP):
                rows_j = lines[n]
                h_j, s_j, k_j, c_j, rho_j, b_j = [rows_j[c : c + 1] for c in range(6)]
                mass = rows_j[6:7] * counts[n]
                push = rows_j[7:8] * counts[n]
                square = jnp.maximum(source[band, n * WIDTH : (n + 1) * WIDTH], TINY)
                at = (GROUP + n) * WIDTH
                closing = source[band, at : at + WIDTH]
                dist = square * lax.rsqrt(square)
                t_i = jnp.maximum(h_i - dist, 0.0)
                t_j = jnp.maximum(h_j - dist, 0.0)
                g_i = t_i * t_i * t_i * s_i
                g_j = t_j * t_j * t_j * s_j
                k = k_i + k_j
                near = k * jnp.minimum(closing, 0.0)
                wide = square + k * k
                top = near * (near - wide * (c_i + c_j)) * (b_i + b_j)
                under = pltpu.reciprocal(wide * wide * (rho_i + rho_j), approx=True)
                v = top * under * (g_i + g_j) * mass
                both = v + g_j * push
                result[0] += both
                for c in range(3):
                    result[1 + c] += both * rows_j[8 + c : 9 + c]
                result[4] += v * closing
            for c in range(5):
                total[cell, c, band, :] = result[c]

    units = count_units(lengths, first, first + HALF)
    begin = (jnp.int32(0), jnp.int32(0))
    distances(begin, d0, WIDTH)

    def half(place, after, d_now, d_next):
        need = sizes[order[place[0]]]
        need = jnp.where(sizes[order[after[0]]] > 64, WIDTH, need)

        def body(rows):
            distances(after, d_next, max(rows, 64))
            pair_terms(place, d_now, rows)

        branch(need, ROWS_ALL, body)

    def step(_, place):
        second = advance(order, lengths, place)
        third = advance(order, lengths, second)
        half(place, second, d0, d1)
        half(second, third, d1, d0)
        return third

    lax.fori_loop(0, (units + 1) // 2, step, begin)

    @pl.loop(0, HALF // 2)
    def _(step):
        for n in range(2):
            cell = step * 2 + n
            pick = chosen[cell].astype(F32)
            back = [
                jnp.sum(
                    jnp.sum(total[cell, c], axis=1, keepdims=True) * pick, axis=0, keepdims=True
                )
                for c in range(5)
            ]
            sums[:, pl.ds(cell, 1), :] = stacked(back).reshape(5, 1, WIDTH)

    here = slice(first, first + HALF)
    alive = live[here, :]
    for c in range(3):
        inner = table[here, c, :] * sums[0] - sums[1 + c]
        accel[c, here, :] = (first_terms[c, here, :] - inner) * alive
    heating[here, :] = (first_terms[3, here, :] + 0.5 * sums[4]) * alive
    if first:
        accel[:, 0:HALF, :] = rest[0][:, 0:HALF, :]
        heating[0:HALF, :] = rest[1][0:HALF, :]


def pack_kernel(positions, velocities, masses, smoothing, energy, counts, active, state, valid, live):
    slot = lax.broadcasted_iota(jnp.int32, (CD, WIDTH), 1)
    held = jnp.where(slot < counts[...], 1.0, 0.0)
    valid[...] = held
    live[...] = jnp.where(active[...] > 0, held, 0.0)
    state[0:3] = positions[...]
    state[3:6] = velocities[...]
    state[M] = masses[...] * held
    state[H] = smoothing[...]
    state[U] = energy[...]


def call(kernel, scalars, arrays, outs, scratch, name, work, limit=48):
    smem = pl.BlockSpec(memory_space=pltpu.SMEM)
    vmem = pl.BlockSpec(memory_space=pltpu.VMEM)
    return pl.pallas_call(
        kernel,
        out_shape=[jax.ShapeDtypeStruct(shape, kind) for shape, kind in outs],
        in_specs=[smem] * len(scalars) + [vmem] * len(arrays),
        out_specs=[vmem] * len(outs),
        scratch_shapes=[pltpu.VMEM(shape, kind) for shape, kind in scratch],
        compiler_params=pltpu.CompilerParams(vmem_limit_bytes=limit * 1024 * 1024),
        cost_estimate=pl.CostEstimate(flops=work, bytes_accessed=2**22, transcendentals=work // 50),
        name=name,
    )(*scalars, *arrays)


def partner_lists(pairs, parts):
    cells = jnp.arange(CD, dtype=jnp.int32)[:, None]
    every = jnp.concatenate([cells, pairs], axis=1)
    slot = jnp.arange(SLOTS, dtype=jnp.int32)
    repeats = jnp.sum((every[:, :, None] == slot).astype(jnp.int32), axis=1)
    taken = jnp.where(repeats > 0, parts[None, :], 0)
    before = (slot[:, None] < slot[None, :]).astype(jnp.int32)
    start = jnp.sum(taken[:, :, None] * before[None], axis=1)
    place = jnp.arange(LIST, dtype=jnp.int32)
    inner = place - start[:, :, None]
    hit = (inner >= 0) & (inner < taken[:, :, None])
    code = PARTS * slot[None, :] + start % PARTS + repeats * 65536
    code = code[:, :, None] + 256 * (PARTS * slot[None, :, None] + inner)
    blank = PARTS * DUMMY * 257
    codes = blank + jnp.sum(jnp.where(hit, code - blank, 0), axis=1)
    codes = jnp.concatenate([codes, jnp.full((1, LIST), blank, jnp.int32)])
    length = (jnp.sum(taken, axis=1) + PARTS - 1) // PARTS
    return length, codes.reshape(-1)


def part_counts(counts, far, requests):
    own = (counts + PART - 1) // PART
    edges = jnp.stack([block[M, :, PART::PART] for block in far])
    theirs = 1 + jnp.sum((edges > 0).astype(jnp.int32), axis=2)
    cell = jnp.arange(CD, dtype=jnp.int32)
    match = jnp.maximum(requests, 0)[:, :, None] == cell
    theirs = jnp.sum(jnp.where(match, theirs[:, None, :], 0), axis=2)
    return jnp.concatenate([own, theirs.reshape(-1)])


def descending(sizes):
    cell = jnp.arange(sizes.shape[0], dtype=jnp.int32)
    ahead = (sizes[None, :] > sizes[:, None]) | (
        (sizes[None, :] == sizes[:, None]) & (cell[None, :] < cell[:, None])
    )
    rank = jnp.sum(ahead.astype(jnp.int32), axis=1)
    return jnp.sum(jnp.where(rank[None, :] == cell[:, None], cell[None, :], 0), axis=1)


def closed(order):
    return jnp.concatenate([order, jnp.full((CD + 1 - order.shape[0],), CD, jnp.int32)])


def on_device(positions, velocities, masses, smoothing, energy, counts, active, requests, pairs):
    state, valid, live = call(
        pack_kernel, (),
        (positions, velocities, masses, smoothing, energy, counts[:, None], active),
        [((9, CD, WIDTH), F32), ((CD, WIDTH), F32), ((CD, WIDTH), F32)],
        [], "pack", 10**5, 60,
    )
    far = [from_ahead(state, d) for d in SHIFTS]
    wanted = requests.reshape(-1)
    lengths, codes = partner_lists(pairs, part_counts(counts, far, requests[0]))
    scalars = (wanted, lengths, codes)
    none = jnp.zeros((1,), jnp.int32)
    count_sizes = jnp.concatenate([counts, none])
    live_sizes = jnp.concatenate([jnp.sum(live, axis=1).astype(jnp.int32), none])

    density, table, right, left = call(
        density_kernel, scalars, (state, *far, masses, valid),
        [((CD, WIDTH), F32), ((TABLE, CHANNELS, WIDTH), F32), ((TABLE * PARTS, 48, WIDTH), BF16),
         ((CD, WIDTH, 48), BF16)],
        [((TABLE * PARTS, 8, WIDTH), F32)] + [((WIDTH, GROUP * WIDTH), F32)] * 2 + [((CD + 1, WIDTH, WIDTH), F32)],
        "density", 10**8,
    )
    rho_far = [from_ahead(density, d) for d in SHIFTS]
    switch, first_terms, smallest = call(
        gradient_kernel, (*scalars, count_sizes, closed(descending(counts))), (table, right, left, density, *rho_far, live),
        [((CD, WIDTH), F32), ((4, CD, WIDTH), F32), ((8, WIDTH), F32)],
        [((TABLE * PARTS, PART, 48), BF16)] + [((WIDTH, GROUP * WIDTH), F32)] * 2
        + [((2 * WIDTH, GROUP * WIDTH), BF16)] * 2
        + [((CD + 1, WIDTH, 48), F32), ((24, CD, WIDTH), F32)],
        "gradient", 10**8,
    )
    packed = jnp.concatenate([switch, smallest], axis=0)
    switch_far = [from_ahead(packed, d) for d in SHIFTS]
    for block in switch_far:
        smallest = jnp.minimum(smallest, block[CD:])
    results = ()
    for half, distances in enumerate(((-7, 7, 14), (-56, -28, 28, 56))):
        blocks = [from_ahead(smallest, d) for d in distances]
        lower = half * HALF
        order = closed(lower + descending(live_sizes[lower : lower + HALF]))
        results = call(
            functools.partial(force_kernel, lower), (*scalars, live_sizes, order),
            (table, right, density, *rho_far, switch, *switch_far, live, first_terms, *results),
            [((3, CD, WIDTH), F32), ((CD, WIDTH), F32)],
            [((TABLE * PARTS, 32, WIDTH), BF16), ((TABLE * PARTS, 16, WIDTH), F32),
             ((HALF, WIDTH, WIDTH), BF16), ((HALF, WIDTH, WIDTH), BF16),
             ((HALF + 1, WIDTH, 8), F32)]
            + [((WIDTH, 2 * GROUP * WIDTH), F32)] * 2
            + [((HALF + 1, 5, WIDTH, WIDTH), F32), ((5, HALF, WIDTH), F32), ((CD, WIDTH), F32)],
            "force", 10**8,
        )
        for block in blocks:
            smallest = jnp.minimum(smallest, block)
    accel, heating = results
    return accel, heating, density, smallest[0, 0]


def solution(mesh):
    in_specs = (
        P(None, "ranks", None),
        P(None, "ranks", None),
        P("ranks", None),
        P("ranks", None),
        P("ranks", None),
        P("ranks"),
        P("ranks", None),
        P("ranks", None, None),
        P("ranks", None),
    )
    out_specs = (P(None, "ranks", None), P("ranks", None), P("ranks", None), P())
    return jax.shard_map(
        on_device, mesh=mesh, in_specs=in_specs, out_specs=out_specs, check_vma=False
    )
```

```python
import functools
import math

import jax
import jax.numpy as jnp
from jax import lax
from jax.experimental import pallas as pl
from jax.experimental.pallas import tpu as pltpu
from jax.sharding import PartitionSpec as P

KERNEL_NORM = 21.0 / (2.0 * math.pi)
ADIABATIC = 5.0 / 3.0
SWITCH_EPS = 0.0001
LARGE_STEP = 10000000000.0
TINY = 1e-12

CD = 32
WIDTH = 128
OFFS = 6
CAP = 4
SLOTS = CD + OFFS * CAP
DUMMY = SLOTS
TABLE = SLOTS + 1
PARTS = 4
PART = WIDTH // PARTS
GROUP = 9
LIST = 27 * PARTS
HALF = CD // 2
ROWS_ALL = (32, 48, 64, 128)
ROWS_VALID = (64, 96, 128)
SHIFTS = (-3, -2, -1, 1, 2, 3)
F32 = jnp.float32
BF16 = jnp.bfloat16

X, V, M, H, U = 0, 3, 6, 7, 8
CHANNELS = 16


def from_ahead(block, distance):
    count = lax.axis_size("ranks")
    route = [((i + distance) % count, i) for i in range(count)]
    return lax.ppermute(block, "ranks", route)


def halves(value):
    high = value.astype(BF16).astype(F32)
    return high, value - high


def thirds(value):
    high, rest = halves(value)
    middle, low = halves(rest)
    return high, middle, low


def stacked(rows):
    return jnp.concatenate(rows, axis=0)


def left_six(value):
    a, b, c = thirds(value)
    return stacked([a, a, b, b, a, c])


def right_six(value):
    a, b, c = thirds(value)
    return stacked([a, b, a, b, c, a])


def dot_rows(left, right):
    return lax.dot_general(left, right, (((1,), (1,)), ((), ())), preferred_element_type=F32)


def dot_plain(left, right):
    return lax.dot_general(left, right, (((1,), (0,)), ((), ())), preferred_element_type=F32)


def each_slot(requests, local, remote):
    @pl.loop(0, CD // 4)
    def _(step):
        for n in range(4):
            local(step * 4 + n)

    for k in range(OFFS):
        for n in range(CAP):
            remote(k, CD + k * CAP + n, jnp.maximum(requests[k * CAP + n], 0))


def advance(order, lengths, place):
    position, index = place
    cell = jnp.minimum(order[position], CD - 1)
    done = index + GROUP >= lengths[cell]
    after = jnp.where(done, position + 1, position)
    return jnp.minimum(after, CD), jnp.where(done, 0, index + GROUP)


def count_units(lengths, low, high):
    def add(cell, total):
        return total + (lengths[cell] + (GROUP - 1)) // GROUP

    return lax.fori_loop(low, high, add, jnp.int32(0))


def entries(codes, cell, index):
    base = cell * LIST + index * PARTS
    found = []
    for n in range(GROUP):
        four = [codes[base + n * PARTS + p] for p in range(PARTS)]
        found.append([(c & 255, (c >> 8) & 255, (c >> 16).astype(F32)) for c in four])
    return found


def part_masks(rows, kind):
    lane = lax.broadcasted_iota(jnp.int32, (rows, WIDTH), 1)
    return [((lane >= PART * p) & (lane < PART * (p + 1))).astype(F32).astype(kind) for p in range(PARTS)]


def tile_of(array, four, masks):
    result = array[four[0][0]] * masks[0]
    for p in range(1, PARTS):
        result += array[four[p][0]] * masks[p]
    return result


def count_line(four):
    lane = lax.broadcasted_iota(jnp.int32, (1, WIDTH), 1)
    result = jnp.full((1, WIDTH), four[0][2], F32)
    for p in range(1, PARTS):
        result = jnp.where(lane >= PART * p, four[p][2], result)
    return result


def side_by_side(array, units, rows):
    masks = part_masks(rows, BF16)
    return jnp.concatenate([tile_of(array, four, masks) for four in units], axis=1)


def turned(value):
    return [value] + [pltpu.roll(value, PART * p, 1) for p in range(1, PARTS)]


def density_kernel(
    requests, lengths, codes, state, far0, far1, far2, far3, far4, far5, own, valid,
    density, table, right, left, weight, d0, d1, total,
):
    far = (far0, far1, far2, far3, far4, far5)

    def fill(source, cell, slot):
        rows = stacked([source[c, pl.ds(cell, 1), :] for c in range(9)])
        place = rows[0:3] - 0.5
        norm = jnp.sum(place * place, axis=0, keepdims=True)
        table[slot] = stacked([place, rows[3:9], jnp.zeros((7, WIDTH), F32)])
        one = jnp.ones((1, WIDTH), F32)
        blank = jnp.zeros((3, WIDTH), F32)
        for p, value in enumerate(turned(stacked([-2.0 * place, one, norm, blank]))):
            right[slot * PARTS + p] = right_six(value).astype(BF16)
        for p, value in enumerate(turned(rows[0:8])):
            weight[slot * PARTS + p] = value
        return place, norm, rows[H : H + 1], one, blank

    def local(s):
        place, norm, length, one, blank = fill(state, s, s)
        scale = 1.0 / (length * length)
        tall = left_six(stacked([place * scale, norm * scale, scale, blank]))
        left[s] = tall.T.astype(BF16)
        total[s] = jnp.zeros((WIDTH, WIDTH), F32)

    each_slot(requests, local, lambda k, s, cell: fill(far[k], cell, s))
    total[CD] = jnp.zeros((WIDTH, WIDTH), F32)
    ones = jnp.ones((1, WIDTH), F32)
    table[DUMMY] = stacked([jnp.zeros((7, WIDTH), F32), ones, ones, jnp.zeros((7, WIDTH), F32)])
    for p in range(PARTS):
        right[DUMMY * PARTS + p] = jnp.zeros((48, WIDTH), BF16)
        weight[DUMMY * PARTS + p] = jnp.zeros((8, WIDTH), F32)

    def distances(place, target):
        cell = jnp.minimum(place[0], CD - 1)
        units = entries(codes, place[0], place[1])
        target[...] = dot_plain(left[cell], side_by_side(right, units, 48))

    masks = part_masks(8, F32)

    def gather(place, source):
        units = entries(codes, place[0], place[1])
        masses = [
            tile_of(weight, four, masks)[M : M + 1, :] * count_line(four) for four in units
        ]
        for start in range(0, WIDTH, 16):
            rows = slice(start, start + 16)
            result = total[place[0], rows, :]
            for n in range(GROUP):
                square = jnp.maximum(source[rows, n * WIDTH : (n + 1) * WIDTH], TINY)
                rest = jnp.maximum(1.0 - square * lax.rsqrt(square), 0.0)
                second = rest * rest
                result += second * second * (1.25 - rest) * masses[n]
            total[place[0], rows, :] = result

    units = count_units(lengths, 0, CD)
    first = (jnp.int32(0), jnp.int32(0))
    distances(first, d0)

    def following(place):
        cell, index = place
        done = index + GROUP >= lengths[jnp.minimum(cell, CD - 1)]
        return jnp.minimum(jnp.where(done, cell + 1, cell), CD), jnp.where(done, 0, index + GROUP)

    def step(_, place):
        second = following(place)
        third = following(second)
        distances(second, d1)
        gather(place, d0)
        distances(third, d0)
        gather(second, d1)
        return third

    lax.fori_loop(0, (units + 1) // 2, step, first)

    @pl.loop(0, CD // 4)
    def _(step):
        for n in range(4):
            cell = step * 4 + n
            density[pl.ds(cell, 1), :] = jnp.sum(total[cell].T, axis=0, keepdims=True)

    length = state[H]
    cube = KERNEL_NORM / (length * length * length)
    density[...] = cube * (4.0 * density[...] + (1.0 - valid[...]) * own[...])


def gradient_kernel(
    requests, lengths, codes, sizes, order, table, right, left, density,
    far0, far1, far2, far3, far4, far5, live,
    switch, first_terms, smallest,
    feature, d0, d1, a0, a1, total, sums,
):
    far = (far0, far1, far2, far3, far4, far5)

    def fill(source, cell, slot):
        rows = table[slot]
        place, speed, mass = rows[0:3], rows[3:6], rows[M : M + 1]
        light = mass / source[pl.ds(cell, 1), :]
        along = jnp.sum(place * speed, axis=0, keepdims=True)
        x, y, z = rows[0:1], rows[1:2], rows[2:3]
        p, q, r = rows[3:4], rows[4:5], rows[5:6]
        cross = stacked([q * z - r * y, r * x - p * z, p * y - q * x])
        one = jnp.ones((1, WIDTH), F32)
        base = stacked([one, place, speed, along])
        whole = stacked([base * light, base * mass, cross * light, jnp.zeros((5, WIDTH), F32)])
        high, low = halves(whole)
        tall = stacked([high, low]).T.astype(BF16)
        for p in range(PARTS):
            feature[slot * PARTS + p] = tall[PART * p : PART * (p + 1)]

    def local(s):
        fill(density, s, s)
        total[s] = jnp.zeros((WIDTH, 48), F32)

    each_slot(requests, local, lambda k, s, cell: fill(far[k], cell, s))
    total[CD] = jnp.zeros((WIDTH, 48), F32)
    for p in range(PARTS):
        feature[DUMMY * PARTS + p] = jnp.zeros((PART, 48), BF16)
    a0[...] = jnp.zeros_like(a0)
    a1[...] = jnp.zeros_like(a1)

    def distances(place, target):
        cell = order[place[0]]
        pair = side_by_side(right, entries(codes, cell, place[1]), 48)
        target[...] = dot_plain(left[jnp.minimum(cell, CD - 1)], pair)

    def collect(place, source, rows):
        cell = order[place[0]]
        units = entries(codes, cell, place[1])
        both = jnp.concatenate([source[0:rows, :], source[WIDTH : WIDTH + rows, :]], axis=0)
        light = jnp.concatenate([feature[e[1]] for four in units for e in four], axis=0)
        both = dot_plain(both, light)
        total[cell, 0:rows, :] += both[:rows] + both[rows:]

    def slopes(place, source, target, rows):
        units = entries(codes, order[place[0]], place[1])
        counts = [jnp.broadcast_to(count_line(four), (16, WIDTH)) for four in units]
        for start in range(0, rows, 16):
            band = slice(start, start + 16)
            below = slice(WIDTH + start, WIDTH + start + 16)
            for n in range(GROUP):
                at = slice(n * WIDTH, (n + 1) * WIDTH)
                square = jnp.maximum(source[band, at], TINY)
                rest = jnp.maximum(1.0 - square * lax.rsqrt(square), 0.0)
                value = rest * rest * (rest * counts[n])
                high = value.astype(BF16)
                target[band, at] = high
                target[below, at] = (value - high.astype(F32)).astype(BF16)

    units = count_units(lengths, 0, CD)
    place = (jnp.int32(0), jnp.int32(0))
    before = (jnp.int32(CD), jnp.int32(0))
    distances(place, d0)

    def half(last, place, after, d_now, d_next, a_last, a_now):
        def body(rows):
            distances(after, d_next)
            collect(last, a_last, rows)
            slopes(place, d_now, a_now, rows)

        branch(jnp.maximum(sizes[order[last[0]]], sizes[order[place[0]]]), ROWS_VALID, body)

    def step(_, carry):
        last, place = carry
        second = advance(order, lengths, place)
        third = advance(order, lengths, second)
        half(last, place, second, d0, d1, a1, a0)
        half(place, second, third, d1, d0, a0, a1)
        return second, third

    last, _ = lax.fori_loop(0, (units + 1) // 2, step, (before, place))
    collect(last, a1, WIDTH)

    @pl.loop(0, CD // 4)
    def _(step):
        for n in range(4):
            cell = step * 4 + n
            tall = total[cell].T
            sums[:, pl.ds(cell, 1), :] = (tall[0:24] + tall[24:48]).reshape(24, 1, WIDTH)

    x = [table[0:CD, c, :] for c in range(3)]
    v = [table[0:CD, 3 + c, :] for c in range(3)]
    length = table[0:CD, H, :]
    energy = table[0:CD, U, :]
    rho = density[...]
    along = x[0] * v[0] + x[1] * v[1] + x[2] * v[2]

    def approach(at):
        value = along * sums[at] + sums[at + 7]
        for c in range(3):
            value = value - x[c] * sums[at + 4 + c] - v[c] * sums[at + 1 + c]
        return value

    square = length * length
    slope = (-20.0 * KERNEL_NORM) / (square * square * length)
    divergence = -slope * approach(0)
    curl = jnp.zeros_like(divergence)
    for c in range(3):
        e, f = (c + 1) % 3, (c + 2) % 3
        part = (
            sums[4 + e] * x[f] - sums[4 + f] * x[e] - sums[16 + c]
            - sums[0] * (v[e] * x[f] - v[f] * x[e])
            + v[e] * sums[1 + f] - v[f] * sums[1 + e]
        )
        curl = curl + part * part
    curl = jnp.sqrt(curl) * jnp.abs(slope)
    sound = jnp.sqrt((ADIABATIC * (ADIABATIC - 1.0)) * energy)
    size = jnp.abs(divergence)
    switch[...] = size / (size + curl + SWITCH_EPS * sound / length)
    ratio = (ADIABATIC - 1.0) * energy / rho * slope
    for c in range(3):
        first_terms[c] = -ratio * (x[c] * sums[8] - sums[9 + c])
    first_terms[3] = ratio * approach(8)
    each = 0.25 * length / (
        sound + 0.6 * (sound + 2.0 * length * jnp.maximum(-divergence, 0.0))
    )
    each = jnp.where(live[...] > 0, each, LARGE_STEP)
    smallest[...] = jnp.broadcast_to(jnp.min(each, keepdims=True), (8, WIDTH))


def branch(need, options, body):
    which = jnp.int32(0)
    for option in options[:-1]:
        which += (need > option).astype(jnp.int32)
    lax.switch(which, [functools.partial(body, option) for option in options])


def force_kernel(
    first, requests, lengths, codes, sizes, order, table, right, density,
    rho0, rho1, rho2, rho3, rho4, rho5, switch, sw0, sw1, sw2, sw3, sw4, sw5, live, first_terms,
    *rest,
):
    accel, heating, other, line, left, chosen, column, d0, d1, total, sums, ranks = rest[-12:]
    rho_far = (rho0, rho1, rho2, rho3, rho4, rho5)
    switch_far = (sw0, sw1, sw2, sw3, sw4, sw5)
    one = jnp.ones((1, WIDTH), F32)

    def fill(rho_source, switch_source, cell, slot):
        rows = table[slot]
        place, speed, mass = rows[0:3], rows[3:6], rows[M : M + 1]
        length, energy = rows[H : H + 1], rows[U : U + 1]
        rho = rho_source[pl.ds(cell, 1), :]
        bulk = switch_source[pl.ds(cell, 1), :]
        along = jnp.sum(place * speed, axis=0, keepdims=True)
        square = length * length
        fourth = square * square
        slope = (-20.0 * KERNEL_NORM) / (fourth * fourth)
        sound = jnp.sqrt((ADIABATIC * (ADIABATIC - 1.0)) * energy)
        push = (ADIABATIC - 1.0) * energy / rho * mass
        values = stacked(
            [length, slope, 0.05 * length, sound * 0.025, rho, 100.0 * bulk, mass, push]
        )
        for p, value in enumerate(turned(stacked([values, place, jnp.zeros((5, WIDTH), F32)]))):
            line[slot * PARTS + p] = value
        for p, value in enumerate(turned(stacked([-speed, -place, one, along]))):
            a, b = halves(value)
            other[slot * PARTS + p] = stacked([a, b, a, b]).astype(BF16)
        return place, speed, along, values

    alive = live[...]
    down = lax.broadcasted_iota(jnp.int32, (WIDTH, WIDTH), 0)
    across = lax.broadcasted_iota(jnp.int32, (WIDTH, WIDTH), 1)
    earlier = jnp.where(down < across, 1.0, 0.0).astype(BF16)
    rank = dot_plain(alive.astype(BF16), earlier)
    ranks[...] = jnp.where(alive > 0, rank, -1.0)

    def slot_only(s):
        fill(density, switch, s, s)

    def local(n):
        s = first + n
        place, speed, along, values = fill(density, switch, s, s)
        norm = jnp.sum(place * place, axis=0, keepdims=True)
        near = left_six(stacked([place, norm, one, jnp.zeros((3, WIDTH), F32)]))
        a, b = halves(stacked([place, speed, along, one]))
        high, middle, low = thirds(values)
        tall = stacked([near, a, a, b, b, high, middle, low, jnp.zeros((24, WIDTH), F32)]).astype(BF16)
        pick = jnp.where(ranks[pl.ds(s, 1), :] == down.astype(F32), 1.0, 0.0).astype(BF16)
        chosen[n] = pick
        spare = 1.0 - jnp.sum(pick.astype(F32), axis=1, keepdims=True)
        moved = dot_rows(pick, tall)
        left[n] = moved.astype(BF16)
        column[n] = moved[:, 80:88] + moved[:, 88:96] + moved[:, 96:104] + spare
        total[n] = jnp.zeros((5, WIDTH, WIDTH), F32)

    @pl.loop(0, HALF // 4)
    def _(step):
        for n in range(4):
            local(step * 4 + n)
            slot_only(HALF - first + step * 4 + n)

    for k in range(OFFS):
        for n in range(CAP):
            cell = jnp.maximum(requests[k * CAP + n], 0)
            fill(rho_far[k], switch_far[k], cell, CD + k * CAP + n)

    total[HALF] = jnp.zeros((5, WIDTH, WIDTH), F32)
    column[HALF] = jnp.ones((WIDTH, 8), F32)
    for p in range(PARTS):
        line[DUMMY * PARTS + p] = jnp.concatenate(
            [jnp.ones((6, WIDTH), F32), jnp.zeros((10, WIDTH), F32)], axis=0
        )
        other[DUMMY * PARTS + p] = jnp.zeros((32, WIDTH), BF16)

    def distances(place, target, rows):
        cell = order[place[0]]
        units = entries(codes, cell, place[1])
        cell = jnp.minimum(cell - first, HALF - 1)
        width = GROUP * WIDTH
        target[0:rows, :width] = dot_plain(left[cell, 0:rows, 0:48], side_by_side(right, units, 48))
        target[0:rows, width:] = dot_plain(left[cell, 0:rows, 48:80], side_by_side(other, units, 32))

    masks = part_masks(16, F32)

    def pair_terms(place, source, rows):
        cell = order[place[0]]
        units = entries(codes, cell, place[1])
        lines = [tile_of(line, four, masks) for four in units]
        counts = [count_line(four) for four in units]
        cell = jnp.minimum(cell - first, HALF)
        for start in range(0, rows, 16):
            band = slice(start, start + 16)
            own = column[cell, band, :]
            h_i, s_i, k_i, c_i, rho_i, b_i = [
                jnp.broadcast_to(own[:, c : c + 1], (16, WIDTH)) for c in range(6)
            ]
            result = [total[cell, c, band, :] for c in range(5)]
            for n in range(GROUP):
                rows_j = lines[n]
                h_j, s_j, k_j, c_j, rho_j, b_j = [rows_j[c : c + 1] for c in range(6)]
                mass = rows_j[6:7] * counts[n]
                push = rows_j[7:8] * counts[n]
                square = jnp.maximum(source[band, n * WIDTH : (n + 1) * WIDTH], TINY)
                at = (GROUP + n) * WIDTH
                closing = source[band, at : at + WIDTH]
                dist = square * lax.rsqrt(square)
                t_i = jnp.maximum(h_i - dist, 0.0)
                t_j = jnp.maximum(h_j - dist, 0.0)
                g_i = t_i * t_i * t_i * s_i
                g_j = t_j * t_j * t_j * s_j
                k = k_i + k_j
                near = k * jnp.minimum(closing, 0.0)
                wide = square + k * k
                top = near * (near - wide * (c_i + c_j)) * (b_i + b_j)
                under = pltpu.reciprocal(wide * wide * (rho_i + rho_j), approx=True)
                v = top * under * (g_i + g_j) * mass
                both = v + g_j * push
                result[0] += both
                for c in range(3):
                    result[1 + c] += both * rows_j[8 + c : 9 + c]
                result[4] += v * closing
            for c in range(5):
                total[cell, c, band, :] = result[c]

    units = count_units(lengths, first, first + HALF)
    begin = (jnp.int32(0), jnp.int32(0))
    distances(begin, d0, WIDTH)

    def half(place, after, d_now, d_next):
        need = sizes[order[place[0]]]
        need = jnp.where(sizes[order[after[0]]] > 64, WIDTH, need)

        def body(rows):
            distances(after, d_next, max(rows, 64))
            pair_terms(place, d_now, rows)

        branch(need, ROWS_ALL, body)

    def step(_, place):
        second = advance(order, lengths, place)
        third = advance(order, lengths, second)
        half(place, second, d0, d1)
        half(second, third, d1, d0)
        return third

    lax.fori_loop(0, (units + 1) // 2, step, begin)

    @pl.loop(0, HALF // 2)
    def _(step):
        for n in range(2):
            cell = step * 2 + n
            pick = chosen[cell].astype(F32)
            back = [
                jnp.sum(
                    jnp.sum(total[cell, c], axis=1, keepdims=True) * pick, axis=0, keepdims=True
                )
                for c in range(5)
            ]
            sums[:, pl.ds(cell, 1), :] = stacked(back).reshape(5, 1, WIDTH)

    here = slice(first, first + HALF)
    alive = live[here, :]
    for c in range(3):
        inner = table[here, c, :] * sums[0] - sums[1 + c]
        accel[c, here, :] = (first_terms[c, here, :] - inner) * alive
    heating[here, :] = (first_terms[3, here, :] + 0.5 * sums[4]) * alive
    if first:
        accel[:, 0:HALF, :] = rest[0][:, 0:HALF, :]
        heating[0:HALF, :] = rest[1][0:HALF, :]


def pack_kernel(counts, positions, velocities, masses, smoothing, energy, active, state, valid, live):
    slot = lax.broadcasted_iota(jnp.int32, (1, WIDTH), 1)
    for cell in range(CD):
        valid[cell : cell + 1, :] = jnp.where(slot < counts[cell], 1.0, 0.0)
    held = valid[...]
    live[...] = jnp.where(active[...] > 0, held, 0.0)
    state[0:3] = positions[...]
    state[3:6] = velocities[...]
    state[M] = masses[...] * held
    state[H] = smoothing[...]
    state[U] = energy[...]


def call(kernel, scalars, arrays, outs, scratch, name, work, limit=48):
    smem = pl.BlockSpec(memory_space=pltpu.SMEM)
    vmem = pl.BlockSpec(memory_space=pltpu.VMEM)
    return pl.pallas_call(
        kernel,
        out_shape=[jax.ShapeDtypeStruct(shape, kind) for shape, kind in outs],
        in_specs=[smem] * len(scalars) + [vmem] * len(arrays),
        out_specs=[vmem] * len(outs),
        scratch_shapes=[pltpu.VMEM(shape, kind) for shape, kind in scratch],
        compiler_params=pltpu.CompilerParams(vmem_limit_bytes=limit * 1024 * 1024),
        cost_estimate=pl.CostEstimate(flops=work, bytes_accessed=2**22, transcendentals=work // 50),
        name=name,
    )(*scalars, *arrays)


def partner_lists(pairs, parts):
    cells = jnp.arange(CD, dtype=jnp.int32)[:, None]
    every = jnp.concatenate([cells, pairs], axis=1)
    slot = jnp.arange(SLOTS, dtype=jnp.int32)
    repeats = jnp.sum((every[:, :, None] == slot).astype(jnp.int32), axis=1)
    taken = jnp.where(repeats > 0, parts[None, :], 0)
    before = (slot[:, None] < slot[None, :]).astype(jnp.int32)
    start = jnp.sum(taken[:, :, None] * before[None], axis=1)
    place = jnp.arange(LIST, dtype=jnp.int32)
    inner = place - start[:, :, None]
    hit = (inner >= 0) & (inner < taken[:, :, None])
    code = PARTS * slot[None, :] + start % PARTS + repeats * 65536
    code = code[:, :, None] + 256 * (PARTS * slot[None, :, None] + inner)
    blank = PARTS * DUMMY * 257
    codes = blank + jnp.sum(jnp.where(hit, code - blank, 0), axis=1)
    codes = jnp.concatenate([codes, jnp.full((1, LIST), blank, jnp.int32)])
    length = (jnp.sum(taken, axis=1) + PARTS - 1) // PARTS
    return length, codes.reshape(-1)


def part_counts(counts, far, requests):
    own = (counts + PART - 1) // PART
    edges = jnp.stack([block[M, :, PART::PART] for block in far])
    theirs = 1 + jnp.sum((edges > 0).astype(jnp.int32), axis=2)
    cell = jnp.arange(CD, dtype=jnp.int32)
    match = jnp.maximum(requests, 0)[:, :, None] == cell
    theirs = jnp.sum(jnp.where(match, theirs[:, None, :], 0), axis=2)
    return jnp.concatenate([own, theirs.reshape(-1)])


def descending(sizes):
    cell = jnp.arange(sizes.shape[0], dtype=jnp.int32)
    ahead = (sizes[None, :] > sizes[:, None]) | (
        (sizes[None, :] == sizes[:, None]) & (cell[None, :] < cell[:, None])
    )
    rank = jnp.sum(ahead.astype(jnp.int32), axis=1)
    return jnp.sum(jnp.where(rank[None, :] == cell[:, None], cell[None, :], 0), axis=1)


def closed(order):
    return jnp.concatenate([order, jnp.full((CD + 1 - order.shape[0],), CD, jnp.int32)])


def on_device(positions, velocities, masses, smoothing, energy, counts, active, requests, pairs):
    state, valid, live = call(
        pack_kernel, (counts,),
        (positions, velocities, masses, smoothing, energy, active),
        [((9, CD, WIDTH), F32), ((CD, WIDTH), F32), ((CD, WIDTH), F32)],
        [], "pack", 10**5, 60,
    )
    far = [from_ahead(state, d) for d in SHIFTS]
    wanted = requests.reshape(-1)
    lengths, codes = partner_lists(pairs, part_counts(counts, far, requests[0]))
    scalars = (wanted, lengths, codes)
    none = jnp.zeros((1,), jnp.int32)
    count_sizes = jnp.concatenate([counts, none])
    live_sizes = jnp.concatenate([jnp.sum(live, axis=1).astype(jnp.int32), none])

    density, table, right, left = call(
        density_kernel, scalars, (state, *far, masses, valid),
        [((CD, WIDTH), F32), ((TABLE, CHANNELS, WIDTH), F32), ((TABLE * PARTS, 48, WIDTH), BF16),
         ((CD, WIDTH, 48), BF16)],
        [((TABLE * PARTS, 8, WIDTH), F32)] + [((WIDTH, GROUP * WIDTH), F32)] * 2 + [((CD + 1, WIDTH, WIDTH), F32)],
        "density", 10**8,
    )
    rho_far = [from_ahead(density, d) for d in SHIFTS]
    switch, first_terms, smallest = call(
        gradient_kernel, (*scalars, count_sizes, closed(descending(counts))), (table, right, left, density, *rho_far, live),
        [((CD, WIDTH), F32), ((4, CD, WIDTH), F32), ((8, WIDTH), F32)],
        [((TABLE * PARTS, PART, 48), BF16)] + [((WIDTH, GROUP * WIDTH), F32)] * 2
        + [((2 * WIDTH, GROUP * WIDTH), BF16)] * 2
        + [((CD + 1, WIDTH, 48), F32), ((24, CD, WIDTH), F32)],
        "gradient", 10**8,
    )
    packed = jnp.concatenate([switch, smallest], axis=0)
    switch_far = [from_ahead(packed, d) for d in SHIFTS]
    for block in switch_far:
        smallest = jnp.minimum(smallest, block[CD:])
    results = ()
    for half, distances in enumerate(((-7, 7, 14), (-56, -28, 28, 56))):
        blocks = [from_ahead(smallest, d) for d in distances]
        lower = half * HALF
        order = closed(lower + descending(live_sizes[lower : lower + HALF]))
        results = call(
            functools.partial(force_kernel, lower), (*scalars, live_sizes, order),
            (table, right, density, *rho_far, switch, *switch_far, live, first_terms, *results),
            [((3, CD, WIDTH), F32), ((CD, WIDTH), F32)],
            [((TABLE * PARTS, 32, WIDTH), BF16), ((TABLE * PARTS, 16, WIDTH), F32),
             ((HALF, WIDTH, WIDTH), BF16), ((HALF, WIDTH, WIDTH), BF16),
             ((HALF + 1, WIDTH, 8), F32)]
            + [((WIDTH, 2 * GROUP * WIDTH), F32)] * 2
            + [((HALF + 1, 5, WIDTH, WIDTH), F32), ((5, HALF, WIDTH), F32), ((CD, WIDTH), F32)],
            "force", 10**8,
        )
        for block in blocks:
            smallest = jnp.minimum(smallest, block)
    accel, heating = results
    return accel, heating, density, smallest[0, 0]


def solution(mesh):
    in_specs = (
        P(None, "ranks", None),
        P(None, "ranks", None),
        P("ranks", None),
        P("ranks", None),
        P("ranks", None),
        P("ranks"),
        P("ranks", None),
        P("ranks", None, None),
        P("ranks", None),
    )
    out_specs = (P(None, "ranks", None), P("ranks", None), P("ranks", None), P())
    return jax.shard_map(
        on_device, mesh=mesh, in_specs=in_specs, out_specs=out_specs, check_vma=False
    )
```
